32 devices in a mesh: seq: 16 (over z, y, x), chan: 2 (over core).
Axes of the slice: x: 2, y: 2, z: 4, core: 2. Of those that a mesh axis runs over, the one named last changes fastest.
Arguments:
- gate_outer: bfloat16 [2048, 4096], P('seq', 'chan'), may hold values from -520 to 520
- gate_inner: bfloat16 [2048, 4096], P('seq', 'chan'), may hold values from -6 to 6
- value_in: bfloat16 [2048, 4096], P('seq', 'chan'), may hold values from -6 to 6
- pole_rates: float32 [8, 4096], P(None, 'chan'), may hold values from 0 to 1, as said below
- pole_weights: float32 [8, 4096], P(None, 'chan'), may hold values from -4 to 4
- skip_gain: float32 [4096], P('chan'), may hold values from -1 to 1
- query_rows: bfloat16 [2048, 4096], P('seq', 'chan'), may hold values from -6 to 6
- key_rows: bfloat16 [2048, 4096], P('seq', 'chan'), may hold values from -6 to 6
Outputs:
- mixed: bfloat16 [2048, 4096], P('seq', 'chan')
The draws below stay inside these ranges and needn't reach their ends.
Inputs may be any that keep to these rules, and one draw needn't show every extreme that they name: `pole_rates`: each rate is positive and at most 1/30.
All inputs are finite; a program needn't handle non-finite values.
Results may differ from the reference program's by a relative error of at most 0.0065.
Values may be sent and summed in bfloat16 or wider, within the bound.
No kernel may reach another device: no remote copies, remote signals or barrier semaphores. Data moves between devices by JAX's collectives and lax.ppermute only.
A program may use at most 128 MiB of HBM per device.

```python
import math
import jax
import jax.numpy as jnp
from jax import lax

HEADS = 32
HD = 128
POLES = 8
CH = 4096
LENGTH = 2048


def draw_query_rows(key, part):
    base_key = jax.random.fold_in(key, 11)
    rows_drawn = jnp.clip(jax.random.normal(base_key, (LENGTH, CH), jnp.float32), -6.0, 6.0)
    return rows_drawn.astype(jnp.bfloat16)


def draw_key_rows(key, part):
    base_key = jax.random.fold_in(key, 12)
    rows_drawn = jnp.clip(jax.random.normal(base_key, (LENGTH, CH), jnp.float32), -6.0, 6.0)
    return rows_drawn.astype(jnp.bfloat16)


def draw_gate_outer(key, part):
    parts_key = jax.random.split(jax.random.fold_in(key, 21), 3)
    column = jnp.arange(CH, dtype=jnp.float32) / CH
    col_scale = jnp.exp(jax.random.uniform(parts_key[1], (1, CH), jnp.float32, 0.0, math.log(10.0)))
    col_scale = col_scale * jnp.exp(0.5 * math.log(3.0) * column)[None, :]
    row_scale = jnp.exp(jax.random.uniform(parts_key[0], (LENGTH, 1), jnp.float32, 0.0, math.log(10.0)))
    noise = jnp.clip(jax.random.normal(parts_key[2], (LENGTH, CH), jnp.float32), -3.0, 3.0)
    corner = 3.0 * 10.0 * 10.0 * math.sqrt(3.0)
    drawn = noise * row_scale * col_scale
    drawn = drawn.at[LENGTH - 1, CH - 1].set(corner)
    return drawn.astype(jnp.bfloat16)


def draw_pole_rates(key, part):
    parts_key = jax.random.split(jax.random.fold_in(key, 31), 3)
    slow = jnp.exp(jax.random.uniform(parts_key[0], (POLES, CH), jnp.float32, math.log(0.2 / LENGTH), math.log(2.0 / LENGTH)))
    fast = jnp.exp(jax.random.uniform(parts_key[1], (POLES, CH), jnp.float32, math.log(1.0 / 50.0), math.log(1.0 / 30.0)))
    share = 0.5
    picked = jax.random.bernoulli(parts_key[2], share, (POLES, CH))
    return jnp.where(picked, slow, fast).astype(jnp.float32)


def shard_levels(own_key, dims, pieces, least, high):
    gain, own = 1.0, jax.random.fold_in(own_key, 6)
    for position, shards_of in pieces:
        heights = jnp.exp(jax.random.uniform(jax.random.fold_in(own, position), (shards_of,), jnp.float32, least / len(pieces), high / len(pieces)))
        gain = gain * jnp.repeat(heights, dims[position] // shards_of).reshape([-1 if axis == position else 1 for axis in range(len(dims))])
    return gain


def gaussian(rng, extent, deviation, bound, pieces=(), kind=jnp.bfloat16):
    loudness = shard_levels(rng, extent, pieces, -0.22, 0.18) if pieces else 1.0
    entries = jax.random.normal(rng, extent, jnp.float32) * deviation * loudness
    return jnp.minimum(jnp.maximum(entries, -bound), bound).astype(kind)


def setup_inputs(seed: int = 0) -> dict:
    seeds = jax.random.split(jax.random.key(seed), 9)
    gate_outer = draw_gate_outer(jax.random.fold_in(seeds[8], 71), 0)
    gate_inner = gaussian(seeds[1], (LENGTH, CH), 1.0, 6.0, ((0, 16), (1, 2)))
    value_in = gaussian(seeds[2], (LENGTH, CH), 1.0, 6.0, ((0, 16), (1, 2)))
    pole_rates = draw_pole_rates(jax.random.fold_in(seeds[8], 71), 0)
    pole_weights = gaussian(seeds[4], (POLES, CH), 1.0, 4.0, ((1, 2),), jnp.float32)
    skip_gain = jnp.clip(jax.random.uniform(seeds[5], (CH,), jnp.float32, -1.0, 1.0) * shard_levels(seeds[5], (CH,), ((0, 2),), -0.4, 0.0), -1.0, 1.0)
    query_rows = draw_query_rows(jax.random.fold_in(seeds[8], 71), 0)
    key_rows = draw_key_rows(jax.random.fold_in(seeds[8], 71), 0)
    return dict(gate_outer=gate_outer, gate_inner=gate_inner, value_in=value_in, pole_rates=pole_rates, pole_weights=pole_weights, skip_gain=skip_gain, query_rows=query_rows, key_rows=key_rows)


def convolve(gated, pole_rates, pole_weights):
    decay = jnp.exp(-pole_rates)
    weighting = pole_weights * jnp.sqrt(pole_rates)

    def advance(modal_state, column):
        modal_state = decay * modal_state + column[None, :]
        return (modal_state, lax.optimization_barrier(jnp.sum(weighting * modal_state, axis=0)))
    start_state = jnp.zeros(pole_rates.shape, jnp.float32)
    final_state, filtered = lax.scan(advance, start_state, gated)
    return filtered

def attend_head(query_head, key_head, value_head):
    total = query_head.shape[0]
    block_rows = min(512, total)
    key_pos = jnp.arange(total, dtype=jnp.int32)
    score_scale = HD ** (-0.5)

    def one_block(block_index):
        first_row = (block_index * block_rows).astype(jnp.int32)
        rows_here = lax.dynamic_slice_in_dim(query_head, first_row, block_rows, 0)
        scores = jnp.dot(rows_here, key_head.T, preferred_element_type=jnp.float32) * score_scale
        query_pos = first_row + jnp.arange(block_rows, dtype=jnp.int32)
        visible = key_pos[None, :] <= query_pos[:, None]
        scores = jnp.where(visible, scores, -1e+30)
        top_score = lax.optimization_barrier(jnp.max(scores, axis=1, keepdims=True))
        expo = jnp.where(visible, jnp.exp(scores - top_score), 0.0)
        totals = lax.optimization_barrier(jnp.sum(expo, axis=1, keepdims=True))
        summed = jnp.dot(expo.astype(jnp.bfloat16), value_head, preferred_element_type=jnp.float32)
        return (summed / totals).astype(jnp.bfloat16)
    blocks = lax.map(one_block, jnp.arange(total // block_rows, dtype=jnp.int32))
    return blocks.reshape(total, value_head.shape[1])

def reference(gate_outer, gate_inner, value_in, pole_rates, pole_weights, skip_gain, query_rows, key_rows):
    gated = gate_inner.astype(jnp.float32) * value_in.astype(jnp.float32)
    filtered = convolve(gated, pole_rates, pole_weights)
    conv_out = gate_outer.astype(jnp.float32) * (filtered + skip_gain[None, :] * gated)
    mean_square = lax.optimization_barrier(jnp.mean(conv_out * conv_out, axis=1, keepdims=True))
    values = (conv_out * lax.rsqrt(mean_square + 1e-06)).astype(jnp.bfloat16)
    total = query_rows.shape[0]

    def per_head(head_index):
        first_col = (head_index * HD).astype(jnp.int32)
        query_head = lax.dynamic_slice_in_dim(query_rows, first_col, HD, 1)
        key_head = lax.dynamic_slice_in_dim(key_rows, first_col, HD, 1)
        value_head = lax.dynamic_slice_in_dim(values, first_col, HD, 1)
        return attend_head(query_head, key_head, value_head)
    outputs = lax.map(per_head, jnp.arange(HEADS, dtype=jnp.int32))
    return jnp.transpose(outputs, (1, 0, 2)).reshape(total, HEADS * HD)
```

```python
import functools
import math

import jax
import jax.numpy as jnp
from jax import lax
from jax.experimental import pallas as pl
from jax.experimental.pallas import tpu as pltpu
from jax.sharding import PartitionSpec as P

HD = 128
LOG2E = math.log2(math.e)
VMEM_CAP = 16 * 1024 * 1024


def call(body, out_shape, flops, moved, exps=0, **kwargs):
    return pl.pallas_call(
        body,
        out_shape=out_shape,
        compiler_params=pltpu.CompilerParams(vmem_limit_bytes=VMEM_CAP),
        cost_estimate=pl.CostEstimate(flops=flops, bytes_accessed=moved, transcendentals=exps),
        **kwargs,
    )


def split_kernel(pieces, per_piece, *refs):
    *ins, out = refs
    rows = ins[0].shape[0]
    for place in range(pieces):
        cols = slice(place * per_piece, (place + 1) * per_piece)
        for which, ref in enumerate(ins):
            out[place, which * rows : (which + 1) * rows, :] = ref[:, cols]


def split_heads(arrays, pieces):
    rows, width = arrays[0].shape
    per_piece = width // pieces
    return call(
        functools.partial(split_kernel, pieces, per_piece),
        jax.ShapeDtypeStruct((pieces, rows * len(arrays), per_piece), arrays[0].dtype),
        0,
        4 * rows * width * len(arrays),
    )(*arrays)


def spread(ref, source, count, groups, pitch):
    for group in range(groups):
        ref[pl.ds(group, count, stride=pitch), :] = source[:, group * HD : (group + 1) * HD]


def local_kernel(groups, pitch, gate, value, rates, weights, skip, out, summary, gated, decay, gain, direct):
    rows = gate.shape[0]
    poles = rates.shape[0]
    if pitch != groups:
        for ref in (gated, decay, gain, direct):
            ref[...] = jnp.zeros_like(ref)
    spread(decay, jnp.exp(-rates[...]), poles, groups, pitch)
    spread(gain, weights[...] * jnp.sqrt(rates[...]), poles, groups, pitch)
    spread(direct, skip[...], 1, groups, pitch)
    for group in range(groups):
        cols = slice(group * HD, (group + 1) * HD)
        product = gate[:, cols].astype(jnp.float32) * value[:, cols].astype(jnp.float32)
        gated[pl.ds(group, rows, stride=pitch), :] = product

    fades = [decay[m * pitch : (m + 1) * pitch, :] for m in range(poles)]
    gains = [gain[m * pitch : (m + 1) * pitch, :] for m in range(poles)]
    own = direct[...]

    def one(t, states):
        at = pl.ds(pl.multiple_of(t * pitch, pitch), pitch)
        now = gated[at, :]
        states = [fade * state + now for fade, state in zip(fades, states)]
        terms = [own * now] + [g * state for g, state in zip(gains, states)]
        while len(terms) > 1:
            terms = [a + b for a, b in zip(terms[::2], terms[1::2])] + terms[len(terms) // 2 * 2 :]
        out[at, :] = terms[0]
        return states

    zero = jnp.zeros((pitch, HD), jnp.float32)
    states = lax.fori_loop(0, rows, one, [zero] * poles, unroll=4)
    for m in range(poles):
        summary[m * pitch : (m + 1) * pitch, :] = states[m]


def local_conv(gate, value, rates, weights, skip, pitch):
    rows, width = gate.shape
    poles = rates.shape[0]
    f32 = jnp.float32
    return call(
        functools.partial(local_kernel, width // HD, pitch),
        (
            jax.ShapeDtypeStruct((rows * pitch, HD), f32),
            jax.ShapeDtypeStruct((poles * pitch, HD), f32),
        ),
        4 * poles * rows * width,
        8 * rows * width,
        scratch_shapes=[
            pltpu.VMEM((rows * pitch, HD), f32),
            pltpu.VMEM((poles * pitch, HD), f32),
            pltpu.VMEM((poles * pitch, HD), f32),
            pltpu.VMEM((pitch, HD), f32),
        ],
    )(gate, value, rates, weights, skip)


def tail_kernel(groups, pitch, local, carry, rates, weights, gate, out, squares, full, decay, gain):
    rows = gate.shape[0]
    poles = rates.shape[0]
    if pitch != groups:
        for ref in (decay, gain):
            ref[...] = jnp.zeros_like(ref)
    spread(decay, jnp.exp(-rates[...]), poles, groups, pitch)
    spread(gain, weights[...] * jnp.sqrt(rates[...]), poles, groups, pitch)
    parts = [slice(m * pitch, (m + 1) * pitch) for m in range(poles)]
    fades = [decay[part, :] for part in parts]

    def one(t, states):
        at = pl.ds(pl.multiple_of(t * pitch, pitch), pitch)
        states = [fade * state for fade, state in zip(fades, states)]
        terms = [local[at, :]] + states
        while len(terms) > 1:
            terms = [a + b for a, b in zip(terms[::2], terms[1::2])] + terms[len(terms) // 2 * 2 :]
        full[at, :] = terms[0]
        return states

    lax.fori_loop(0, rows, one, [gain[part, :] * carry[part, :] for part in parts], unroll=4)
    total = jnp.zeros((rows, HD), jnp.float32)
    for group in range(groups):
        cols = slice(group * HD, (group + 1) * HD)
        conv = gate[:, cols].astype(jnp.float32) * full[pl.ds(group, rows, stride=pitch), :]
        out[group] = conv
        total = total + conv * conv
    ones = jnp.ones((8, HD), jnp.float32)
    summed = lax.dot_general(
        ones,
        total,
        (((1,), (1,)), ((), ())),
        precision=lax.Precision.HIGHEST,
        preferred_element_type=jnp.float32,
    )
    squares[...] = summed[0:1, :]


def tail_conv(local, carry, rates, weights, gate, pitch):
    rows, width = gate.shape
    poles = rates.shape[0]
    f32 = jnp.float32
    return call(
        functools.partial(tail_kernel, width // HD, pitch),
        (
            jax.ShapeDtypeStruct((width // HD, rows, HD), f32),
            jax.ShapeDtypeStruct((1, rows), f32),
        ),
        3 * poles * rows * width,
        10 * rows * width,
        scratch_shapes=[
            pltpu.VMEM((rows * pitch, HD), f32),
            pltpu.VMEM((poles * pitch, HD), f32),
            pltpu.VMEM((poles * pitch, HD), f32),
        ],
    )(local, carry, rates, weights, gate)


def norm_kernel(channels, conv, squares, out):
    rows = conv.shape[1]
    scale = lax.rsqrt(squares[...] / channels + 1e-06)
    scale = jnp.transpose(jnp.broadcast_to(scale, (HD, rows)))
    per_chunk = out.shape[2] // HD
    for group in range(conv.shape[0]):
        place, inner = divmod(group, per_chunk)
        out[place, :, inner * HD : (inner + 1) * HD] = (conv[group] * scale).astype(out.dtype)


def normalize(conv, squares, channels, pieces):
    groups, rows, _ = conv.shape
    return call(
        functools.partial(norm_kernel, channels),
        jax.ShapeDtypeStruct((pieces, rows, groups // pieces * HD), jnp.bfloat16),
        groups * rows * HD,
        6 * groups * rows * HD,
    )(conv, squares)


def prefix_state(summary, rates, block_rows, axis):
    size = lax.axis_size(axis)
    place = lax.axis_index(axis)
    span = rates * jnp.float32(block_rows)
    total, before = summary, jnp.zeros_like(summary)
    step = 1
    while step < size:
        many = min(4, size // step)
        mine = place // step % many
        inside = place % step
        others = [
            lax.ppermute(total, axis, [(i, i ^ (step * k)) for i in range(size)])
            for k in range(1, many)
        ]
        new_total = jnp.exp(-span * (step * (many - 1 - mine)).astype(jnp.float32)) * total
        for k, other in enumerate(others, 1):
            its = mine ^ k
            gap = ((mine - 1 - its) * step + inside).astype(jnp.float32)
            fade = jnp.exp(-span * jnp.maximum(gap, 0.0))
            before = before + jnp.where(its < mine, fade * other, 0.0)
            fade = jnp.exp(-span * (step * (many - 1 - its)).astype(jnp.float32))
            new_total = new_total + fade * other
        total = new_total
        step *= many
    return before


def score_kernel(block, inputs, weights, totals, scores):
    chunks, twice, _ = inputs.shape
    rows = twice // 2
    per_block = block // rows
    factor = LOG2E * HD ** (-0.5)
    row = lax.broadcasted_iota(jnp.int32, (block, block), 0)
    col = lax.broadcasted_iota(jnp.int32, (block, block), 1)
    visible = col <= row
    for turn in range(chunks // per_block):
        query = inputs[turn * per_block : (turn + 1) * per_block, 0:rows, :].reshape(block, HD)
        top = None
        for part in range(turn + 1):
            key = inputs[part * per_block : (part + 1) * per_block, rows:, :].reshape(block, HD)
            got = lax.dot_general(
                query, key, (((1,), (1,)), ((), ())), preferred_element_type=jnp.float32
            )
            if part == turn:
                got = jnp.where(visible, got, -1e30)
            scores[:, part * block : (part + 1) * block] = got
            for lane in range(0, block, HD):
                one = got[:, lane : lane + HD]
                top = one if top is None else jnp.maximum(top, one)
        top = jnp.max(top, axis=1, keepdims=True) * factor
        summed = jnp.zeros((block, HD), jnp.float32)
        for part in range(turn + 1):
            expo = jnp.exp2(scores[:, part * block : (part + 1) * block] * factor - top)
            for lane in range(0, block, HD):
                summed = summed + expo[:, lane : lane + HD]
            weights[turn * (turn + 1) // 2 + part] = expo.astype(jnp.bfloat16)
        total = jnp.sum(summed, axis=1, keepdims=True)
        totals[turn * block : (turn + 1) * block, :] = jnp.broadcast_to(total, (block, HD))


def mix_kernel(block, weights, totals, values, out):
    chunks, rows, _ = values.shape
    per_block = block // rows
    for turn in range(chunks // per_block):
        mixed = jnp.zeros((block, HD), jnp.float32)
        for part in range(turn + 1):
            value = values[part * per_block : (part + 1) * per_block].reshape(block, HD)
            mixed = mixed + jnp.dot(
                weights[turn * (turn + 1) // 2 + part], value, preferred_element_type=jnp.float32
            )
        mixed = mixed / totals[turn * block : (turn + 1) * block, :]
        out[turn * per_block : (turn + 1) * per_block] = mixed.astype(out.dtype).reshape(
            per_block, rows, HD
        )


def block_of(chunks, rows):
    block = rows
    while block < 256 and chunks * rows % (2 * block) == 0:
        block *= 2
    return block


def head_weights(pair):
    chunks, twice, _ = pair.shape
    length = chunks * twice // 2
    block = block_of(chunks, twice // 2)
    tiles = (length // block) * (length // block + 1) // 2
    return call(
        functools.partial(score_kernel, block),
        (
            jax.ShapeDtypeStruct((tiles, block, block), jnp.bfloat16),
            jax.ShapeDtypeStruct((length, HD), jnp.float32),
        ),
        tiles * block * block * (2 * HD + 8),
        tiles * block * block * 2,
        tiles * block * block,
        scratch_shapes=[pltpu.VMEM((block, length), jnp.float32)],
    )(pair)


def head_mix(weights, totals, values):
    chunks, rows, _ = values.shape
    block = block_of(chunks, rows)
    return call(
        functools.partial(mix_kernel, block),
        jax.ShapeDtypeStruct((chunks, rows, HD), jnp.bfloat16),
        weights.size * 2 * HD,
        weights.size * 2,
    )(weights, totals, values)


def gathered_head(query, key, value, first_row):
    count, step = key.shape[0], math.gcd(key.shape[0], 1024)
    query_pos = first_row + jnp.arange(query.shape[0], dtype=jnp.int32)

    def one(turn, carried):
        top, total, mixed = carried
        keys = lax.dynamic_slice_in_dim(key, turn * step, step, 0)
        values = lax.dynamic_slice_in_dim(value, turn * step, step, 0)
        scores = jnp.dot(query, keys.T, preferred_element_type=jnp.float32) * HD ** (-0.5)
        visible = (turn * step + jnp.arange(step, dtype=jnp.int32))[None, :] <= query_pos[:, None]
        scores = jnp.where(visible, scores, -1e30)
        new_top = jnp.maximum(top, jnp.max(scores, axis=1, keepdims=True))
        rescale = jnp.exp(top - new_top)
        expo = jnp.where(visible, jnp.exp(scores - new_top), 0.0)
        total = total * rescale + jnp.sum(expo, axis=1, keepdims=True)
        part = jnp.dot(expo.astype(jnp.bfloat16), values, preferred_element_type=jnp.float32)
        return new_top, total, mixed * rescale + part

    rows = query.shape[0]
    start = (
        jnp.full((rows, 1), -1e30, jnp.float32),
        jnp.zeros((rows, 1), jnp.float32),
        jnp.zeros((rows, HD), jnp.float32),
    )
    _, total, mixed = lax.fori_loop(0, count // step, one, start)
    return (mixed / total).astype(jnp.bfloat16)


def local(
    gate_outer, gate_inner, value_in, pole_rates, pole_weights, skip_gain, query_rows, key_rows
):
    rows, width = gate_outer.shape
    heads = width // HD
    size = lax.axis_size("seq")
    channels = width * lax.axis_size("chan")
    group_count = size // heads
    groups = None
    if group_count > 1:
        groups = [list(range(g * heads, (g + 1) * heads)) for g in range(group_count)]
    exchange = functools.partial(
        lax.all_to_all, axis_name="seq", split_axis=0, concat_axis=0, axis_index_groups=groups
    )
    pitch = -(-heads // 8) * 8

    pair = exchange(split_heads([query_rows, key_rows], heads))
    part, summary = local_conv(
        gate_inner, value_in, pole_rates, pole_weights, skip_gain[None, :], pitch
    )
    spread_rates = pole_rates.reshape(-1, heads, HD)
    spread_rates = jnp.pad(spread_rates, ((0, 0), (0, pitch - heads), (0, 0))).reshape(-1, HD)
    carry = prefix_state(summary, spread_rates, rows, "seq")
    conv, squares = tail_conv(part, carry, pole_rates, pole_weights, gate_outer, pitch)
    values = exchange(normalize(conv, lax.psum(squares, "chan"), channels, heads))
    if group_count == 1:
        weights, totals = head_weights(pair)
        mixed = head_mix(weights, totals, values)
    else:
        mine = lax.axis_index("seq") // heads
        others = [list(range(h, size, heads)) for h in range(heads)]
        gather = functools.partial(
            lax.all_gather, axis_name="seq", axis_index_groups=others, tiled=True
        )
        span = heads * rows
        mixed = gathered_head(
            pair[:, :rows].reshape(span, HD),
            gather(pair[:, rows:].reshape(span, HD)),
            gather(values.reshape(span, HD)),
            mine * span,
        ).reshape(heads, rows, HD)
    return jnp.transpose(exchange(mixed), (1, 0, 2)).reshape(rows, width)


def solution(mesh):
    rows = P("seq", "chan")
    poles = P(None, "chan")
    return jax.shard_map(
        local,
        mesh=mesh,
        in_specs=(rows, rows, rows, poles, poles, P("chan"), rows, rows),
        out_specs=rows,
        check_vma=False,
    )
```

```python
import functools
import math

import jax
import jax.numpy as jnp
from jax import lax
from jax.experimental import pallas as pl
from jax.experimental.pallas import tpu as pltpu
from jax.sharding import PartitionSpec as P

HD = 128
LOG2E = math.log2(math.e)
HBM = pl.BlockSpec(memory_space=pltpu.HBM)
VMEM = pl.BlockSpec(memory_space=pltpu.VMEM)


def far(array):
    return pltpu.with_memory_space_constraint(array, pltpu.HBM)


def near(array):
    return pltpu.with_memory_space_constraint(array, pltpu.VMEM)
VMEM_CAP = 12 * 1024 * 1024


def call(body, out_shape, flops, moved, exps=0, **kwargs):
    return pl.pallas_call(
        body,
        out_shape=out_shape,
        compiler_params=pltpu.CompilerParams(vmem_limit_bytes=VMEM_CAP),
        cost_estimate=pl.CostEstimate(flops=flops, bytes_accessed=moved, transcendentals=exps),
        **kwargs,
    )


def run_copies(copies):
    for copy in copies:
        copy.start()
    for copy in copies:
        copy.wait()


def join_kernel(source, out, done):
    pieces, _, wide = source.shape
    run_copies(
        [
            pltpu.make_async_copy(source.at[i], out.at[:, pl.ds(i * wide, wide)], done.at[i])
            for i in range(pieces)
        ]
    )


def join_heads(array):
    pieces, rows, wide = array.shape
    return call(
        join_kernel,
        pltpu.HBM((rows, pieces * wide), array.dtype),
        0,
        4 * rows * pieces * wide,
        in_specs=[VMEM],
        out_specs=HBM,
        scratch_shapes=[pltpu.SemaphoreType.DMA((pieces,))],
    )(array)


def spread(ref, source, count, groups, pitch):
    for group in range(groups):
        ref[pl.ds(group, count, stride=pitch), :] = source[:, group * HD : (group + 1) * HD]


def first_kernel(groups, pitch, *refs):
    gate_far, value_far, rates_far, weights_far, skip_far, query_far, key_far = refs[:7]
    out, summary, pair = refs[7:10]
    (gated, decay, gain, direct, gate, value, rates, weights, skip, query, key) = refs[10:21]
    small, large, staged, moved = refs[21:]
    rows = gate.shape[0]
    poles = rates.shape[0]
    parts = gate.shape[1] // large.shape[1]
    pieces, _, wide = pair.shape
    parameters = [
        pltpu.make_async_copy(source, target, small.at[i])
        for i, (source, target) in enumerate(
            [(rates_far, rates), (weights_far, weights), (skip_far, skip)]
        )
    ]
    streams = []
    for i in range(large.shape[1]):
        cols = pl.ds(i * parts, parts)
        for which, (source, target) in enumerate([(gate_far, gate), (value_far, value)]):
            streams.append(
                pltpu.make_async_copy(source.at[:, cols], target.at[:, cols], large.at[which, i])
            )
    stages, moves = [], []
    for which, (source, middle) in enumerate([(query_far, query), (key_far, key)]):
        stages.append(pltpu.make_async_copy(source, middle, staged.at[which]))
        for i in range(pieces):
            cols = pl.ds(i * wide, wide)
            moves.append(
                pltpu.make_async_copy(
                    middle.at[:, cols], pair.at[i, pl.ds(which * rows, rows)], moved.at[which, i]
                )
            )
    for copy in parameters + streams + stages:
        copy.start()
    if pitch != groups:
        for ref in (gated, decay, gain, direct):
            ref[...] = jnp.zeros_like(ref)
    for copy in parameters:
        copy.wait()
    spread(decay, jnp.exp(-rates[...]), poles, groups, pitch)
    spread(gain, weights[...] * jnp.sqrt(rates[...]), poles, groups, pitch)
    spread(direct, skip[...], 1, groups, pitch)
    for group in range(groups):
        if group * HD % parts == 0:
            for copy in streams[2 * (group * HD // parts) :][:2]:
                copy.wait()
        cols = slice(group * HD, (group + 1) * HD)
        product = gate[:, cols].astype(jnp.float32) * value[:, cols].astype(jnp.float32)
        gated[pl.ds(group, rows, stride=pitch), :] = product

    for copy in stages:
        copy.wait()
    for copy in moves:
        copy.start()

    fades = [decay[m * pitch : (m + 1) * pitch, :] for m in range(poles)]
    gains = [gain[m * pitch : (m + 1) * pitch, :] for m in range(poles)]
    own = direct[...]

    def one(t, states):
        at = pl.ds(pl.multiple_of(t * pitch, pitch), pitch)
        now = gated[at, :]
        states = [fade * state + now for fade, state in zip(fades, states)]
        terms = [own * now] + [g * state for g, state in zip(gains, states)]
        while len(terms) > 1:
            terms = [a + b for a, b in zip(terms[::2], terms[1::2])] + terms[len(terms) // 2 * 2 :]
        out[at, :] = terms[0]
        return states

    zero = jnp.zeros((pitch, HD), jnp.float32)
    states = lax.fori_loop(0, rows, one, [zero] * poles, unroll=4)
    for m in range(poles):
        summary[m * pitch : (m + 1) * pitch, :] = states[m]
    for copy in moves:
        copy.wait()


def first(gate, value, rates, weights, skip, query, key, pitch):
    rows, width = gate.shape
    poles = rates.shape[0]
    heads = width // HD
    streams = 4 if heads % 4 == 0 else 1
    f32 = jnp.float32
    return call(
        functools.partial(first_kernel, heads, pitch),
        (
            jax.ShapeDtypeStruct((rows * pitch, HD), f32),
            jax.ShapeDtypeStruct((poles * pitch, HD), f32),
            pltpu.HBM((heads, 2 * rows, HD), key.dtype),
        ),
        4 * poles * rows * width,
        16 * rows * width,
        in_specs=[HBM] * 7,
        out_specs=(VMEM, VMEM, HBM),
        scratch_shapes=[
            pltpu.VMEM((rows * pitch, HD), f32),
            pltpu.VMEM((poles * pitch, HD), f32),
            pltpu.VMEM((poles * pitch, HD), f32),
            pltpu.VMEM((pitch, HD), f32),
            pltpu.VMEM((rows, width), gate.dtype),
            pltpu.VMEM((rows, width), value.dtype),
            pltpu.VMEM(rates.shape, f32),
            pltpu.VMEM(weights.shape, f32),
            pltpu.VMEM(skip.shape, f32),
            pltpu.VMEM((rows, width), query.dtype),
            pltpu.VMEM((rows, width), key.dtype),
            pltpu.SemaphoreType.DMA((3,)),
            pltpu.SemaphoreType.DMA((2, streams)),
            pltpu.SemaphoreType.DMA((2,)),
            pltpu.SemaphoreType.DMA((2, heads)),
        ],
    )(*map(far, (gate, value, rates, weights, skip, query, key)))


def tail_kernel(
    groups, pitch, local, carry, rates, weights, gate_far, out, squares, full, decay, gain, gate, done
):
    rows = gate.shape[0]
    fetch = pltpu.make_async_copy(gate_far, gate, done)
    fetch.start()
    poles = rates.shape[0]
    if pitch != groups:
        for ref in (decay, gain):
            ref[...] = jnp.zeros_like(ref)
    spread(decay, jnp.exp(-rates[...]), poles, groups, pitch)
    spread(gain, weights[...] * jnp.sqrt(rates[...]), poles, groups, pitch)
    parts = [slice(m * pitch, (m + 1) * pitch) for m in range(poles)]
    fades = [decay[part, :] for part in parts]

    def one(t, states):
        at = pl.ds(pl.multiple_of(t * pitch, pitch), pitch)
        states = [fade * state for fade, state in zip(fades, states)]
        terms = [local[at, :]] + states
        while len(terms) > 1:
            terms = [a + b for a, b in zip(terms[::2], terms[1::2])] + terms[len(terms) // 2 * 2 :]
        full[at, :] = terms[0]
        return states

    lax.fori_loop(0, rows, one, [gain[part, :] * carry[part, :] for part in parts], unroll=4)
    fetch.wait()
    total = jnp.zeros((rows, HD), jnp.float32)
    for group in range(groups):
        cols = slice(group * HD, (group + 1) * HD)
        conv = gate[:, cols].astype(jnp.float32) * full[pl.ds(group, rows, stride=pitch), :]
        out[group] = conv
        total = total + conv * conv
    ones = jnp.ones((8, HD), jnp.float32)
    summed = lax.dot_general(
        ones,
        total,
        (((1,), (1,)), ((), ())),
        precision=lax.Precision.HIGHEST,
        preferred_element_type=jnp.float32,
    )
    squares[...] = summed[0:1, :]


def tail_conv(local, carry, rates, weights, gate, pitch):
    rows, width = gate.shape
    poles = rates.shape[0]
    f32 = jnp.float32
    return call(
        functools.partial(tail_kernel, width // HD, pitch),
        (
            jax.ShapeDtypeStruct((width // HD, rows, HD), f32),
            jax.ShapeDtypeStruct((1, rows), f32),
        ),
        4700 * poles * rows * width,
        10 * rows * width,
        in_specs=[VMEM, VMEM, VMEM, VMEM, HBM],
        scratch_shapes=[
            pltpu.VMEM((rows * pitch, HD), f32),
            pltpu.VMEM((poles * pitch, HD), f32),
            pltpu.VMEM((poles * pitch, HD), f32),
            pltpu.VMEM((rows, width), gate.dtype),
            pltpu.SemaphoreType.DMA,
        ],
    )(local, carry, rates, weights, far(gate))


def norm_kernel(channels, conv, squares, out):
    rows = conv.shape[1]
    scale = lax.rsqrt(squares[...] / channels + 1e-06)
    scale = jnp.transpose(jnp.broadcast_to(scale, (HD, rows)))
    per_chunk = out.shape[2] // HD
    for group in range(conv.shape[0]):
        place, inner = divmod(group, per_chunk)
        out[place, :, inner * HD : (inner + 1) * HD] = (conv[group] * scale).astype(out.dtype)


def normalize(conv, squares, channels, pieces):
    groups, rows, _ = conv.shape
    return call(
        functools.partial(norm_kernel, channels),
        jax.ShapeDtypeStruct((pieces, rows, groups // pieces * HD), jnp.bfloat16),
        groups * rows * HD,
        6 * groups * rows * HD,
    )(conv, squares)


def prefix_state(summary, rates, block_rows, axis):
    size = lax.axis_size(axis)
    place = lax.axis_index(axis)
    span = rates * jnp.float32(block_rows)

    def fade(blocks):
        return jnp.exp(-span * jnp.maximum(blocks, 0).astype(jnp.float32))

    strides = [1]
    while strides[-1] * 4 < size:
        strides.append(strides[-1] * 4)
    before, above = None, size
    for stride in reversed(strides):
        many = above // stride
        digit, inside = place // stride % many, place % above
        total = None if before is None else fade(digit * stride) * before
        for k in range(1, many):
            other = digit ^ k
            gap = other * stride - inside - 1
            sent = summary
            if before is not None:
                sent = fade(other * stride) * before + jnp.where(
                    digit < other, fade(gap) * summary, 0.0
                )
            got = lax.ppermute(sent, axis, [(i, i ^ (stride * k)) for i in range(size)])
            if before is None:
                gap = digit * stride - (inside - digit * stride + other * stride) - 1
                got = jnp.where(other < digit, fade(gap) * got, 0.0)
            total = got if total is None else total + got
        before, above = total, stride
    return before


def score_kernel(block, pair, weights, totals, scores, packed, sent):
    chunks, twice, _ = pair.shape
    rows = twice // 2
    per_block = block // rows
    factor = LOG2E * HD ** (-0.5)
    row = lax.broadcasted_iota(jnp.int32, (block, block), 0)
    col = lax.broadcasted_iota(jnp.int32, (block, block), 1)
    visible = col <= row
    sending = []
    for turn in range(chunks // per_block):
        query = pair[turn * per_block : (turn + 1) * per_block, 0:rows].reshape(block, HD)
        top = None
        for part in range(turn + 1):
            key = pair[part * per_block : (part + 1) * per_block, rows:].reshape(block, HD)
            got = lax.dot_general(
                query, key, (((1,), (1,)), ((), ())), preferred_element_type=jnp.float32
            )
            if part == turn:
                got = jnp.where(visible, got, -1e30)
            scores[:, part * block : (part + 1) * block] = got
            for lane in range(0, block, HD):
                one = got[:, lane : lane + HD]
                top = one if top is None else jnp.maximum(top, one)
        top = jnp.max(top, axis=1, keepdims=True) * factor
        summed = jnp.zeros((block, HD), jnp.float32)
        first = turn * (turn + 1) // 2
        for part in range(turn + 1):
            expo = jnp.exp2(scores[:, part * block : (part + 1) * block] * factor - top)
            for lane in range(0, block, HD):
                summed = summed + expo[:, lane : lane + HD]
            packed[first + part] = expo.astype(jnp.bfloat16)
        total = jnp.sum(summed, axis=1, keepdims=True)
        totals[turn * block : (turn + 1) * block, :] = jnp.broadcast_to(total, (block, HD))
        tiles = pl.ds(first, turn + 1)
        sending.append(pltpu.make_async_copy(packed.at[tiles], weights.at[tiles], sent.at[turn]))
        sending[-1].start()
    for copy in sending:
        copy.wait()


def mix_kernel(block, weights, totals, values, out, packed, got):
    chunks, rows, _ = values.shape
    per_block = block // rows
    coming = []
    for turn in range(chunks // per_block):
        tiles = pl.ds(turn * (turn + 1) // 2, turn + 1)
        coming.append(pltpu.make_async_copy(weights.at[tiles], packed.at[tiles], got.at[turn]))
        coming[-1].start()
    for turn in range(chunks // per_block):
        coming[turn].wait()
        mixed = jnp.zeros((block, HD), jnp.float32)
        for part in range(turn + 1):
            value = values[part * per_block : (part + 1) * per_block].reshape(block, HD)
            mixed = mixed + jnp.dot(
                packed[turn * (turn + 1) // 2 + part], value, preferred_element_type=jnp.float32
            )
        mixed = mixed / totals[turn * block : (turn + 1) * block, :]
        out[turn * per_block : (turn + 1) * per_block] = mixed.astype(out.dtype).reshape(
            per_block, rows, HD
        )


def block_of(chunks, rows):
    block = rows
    while block < 256 and chunks * rows % (2 * block) == 0:
        block *= 2
    return block


def head_weights(pair):
    chunks, twice, _ = pair.shape
    rows = twice // 2
    length = chunks * rows
    block = block_of(chunks, rows)
    turns = length // block
    tiles = turns * (turns + 1) // 2
    return call(
        functools.partial(score_kernel, block),
        (
            pltpu.HBM((tiles, block, block), jnp.bfloat16),
            jax.ShapeDtypeStruct((length, HD), jnp.float32),
        ),
        tiles * block * block * (2 * HD + 8),
        tiles * block * block * 2,
        tiles * block * block,
        out_specs=(HBM, VMEM),
        scratch_shapes=[
            pltpu.VMEM((block, length), jnp.float32),
            pltpu.VMEM((tiles, block, block), jnp.bfloat16),
            pltpu.SemaphoreType.DMA((turns,)),
        ],
    )(pair)


def head_mix(weights, totals, values):
    chunks, rows, _ = values.shape
    block = block_of(chunks, rows)
    return call(
        functools.partial(mix_kernel, block),
        jax.ShapeDtypeStruct((chunks, rows, HD), jnp.bfloat16),
        weights.size * 2 * HD,
        weights.size * 2,
        in_specs=[HBM, VMEM, VMEM],
        scratch_shapes=[
            pltpu.VMEM(weights.shape, weights.dtype),
            pltpu.SemaphoreType.DMA((chunks * rows // block,)),
        ],
    )(far(weights), totals, values)


def gathered_head(query, key, value, first_row):
    count, step = key.shape[0], math.gcd(key.shape[0], 1024)
    query_pos = first_row + jnp.arange(query.shape[0], dtype=jnp.int32)

    def one(turn, carried):
        top, total, mixed = carried
        keys = lax.dynamic_slice_in_dim(key, turn * step, step, 0)
        values = lax.dynamic_slice_in_dim(value, turn * step, step, 0)
        scores = jnp.dot(query, keys.T, preferred_element_type=jnp.float32) * HD ** (-0.5)
        visible = (turn * step + jnp.arange(step, dtype=jnp.int32))[None, :] <= query_pos[:, None]
        scores = jnp.where(visible, scores, -1e30)
        new_top = jnp.maximum(top, jnp.max(scores, axis=1, keepdims=True))
        rescale = jnp.exp(top - new_top)
        expo = jnp.where(visible, jnp.exp(scores - new_top), 0.0)
        total = total * rescale + jnp.sum(expo, axis=1, keepdims=True)
        part = jnp.dot(expo.astype(jnp.bfloat16), values, preferred_element_type=jnp.float32)
        return new_top, total, mixed * rescale + part

    rows = query.shape[0]
    start = (
        jnp.full((rows, 1), -1e30, jnp.float32),
        jnp.zeros((rows, 1), jnp.float32),
        jnp.zeros((rows, HD), jnp.float32),
    )
    _, total, mixed = lax.fori_loop(0, count // step, one, start)
    return (mixed / total).astype(jnp.bfloat16)


def local(
    gate_outer, gate_inner, value_in, pole_rates, pole_weights, skip_gain, query_rows, key_rows
):
    rows, width = gate_outer.shape
    heads = width // HD
    size = lax.axis_size("seq")
    channels = width * lax.axis_size("chan")
    group_count = size // heads
    groups = None
    if group_count > 1:
        groups = [list(range(g * heads, (g + 1) * heads)) for g in range(group_count)]
    exchange = functools.partial(
        lax.all_to_all, axis_name="seq", split_axis=0, concat_axis=0, axis_index_groups=groups
    )
    pitch = -(-heads // 8) * 8

    part, summary, chunks = first(
        gate_inner, value_in, pole_rates, pole_weights, skip_gain[None, :], query_rows, key_rows, pitch
    )
    pair = exchange(chunks)
    spread_rates = pole_rates.reshape(-1, heads, HD)
    spread_rates = jnp.pad(spread_rates, ((0, 0), (0, pitch - heads), (0, 0))).reshape(-1, HD)
    carry = prefix_state(summary, spread_rates, rows, "seq")
    conv, squares = tail_conv(part, carry, pole_rates, pole_weights, gate_outer, pitch)
    values = exchange(normalize(conv, lax.psum(squares, "chan"), channels, heads))
    if group_count == 1:
        weights, totals = head_weights(pair)
        mixed = head_mix(weights, totals, values)
    else:
        mine = lax.axis_index("seq") // heads
        others = [list(range(h, size, heads)) for h in range(heads)]
        gather = functools.partial(
            lax.all_gather, axis_name="seq", axis_index_groups=others, tiled=True
        )
        span = heads * rows
        mixed = gathered_head(
            pair[:, :rows].reshape(span, HD),
            gather(pair[:, rows:].reshape(span, HD)),
            gather(values.reshape(span, HD)),
            mine * span,
        ).reshape(heads, rows, HD)
    return join_heads(exchange(mixed))


def solution(mesh):
    rows = P("seq", "chan")
    poles = P(None, "chan")
    return jax.shard_map(
        local,
        mesh=mesh,
        in_specs=(rows, rows, rows, poles, poles, P("chan"), rows, rows),
        out_specs=rows,
        check_vma=False,
    )
```

```python
import functools
import math

import jax
import jax.numpy as jnp
from jax import lax
from jax.experimental import pallas as pl
from jax.experimental.pallas import tpu as pltpu
from jax.sharding import PartitionSpec as P

HD = 128
LOG2E = math.log2(math.e)
PLANE = 4
HBM = pl.BlockSpec(memory_space=pltpu.HBM)
VMEM = pl.BlockSpec(memory_space=pltpu.VMEM)


def far(array):
    return pltpu.with_memory_space_constraint(array, pltpu.HBM)


def near(array):
    return pltpu.with_memory_space_constraint(array, pltpu.VMEM)
VMEM_CAP = 12 * 1024 * 1024


def call(body, out_shape, flops, moved, exps=0, **kwargs):
    return pl.pallas_call(
        body,
        out_shape=out_shape,
        compiler_params=pltpu.CompilerParams(vmem_limit_bytes=VMEM_CAP),
        cost_estimate=pl.CostEstimate(flops=flops, bytes_accessed=moved, transcendentals=exps),
        **kwargs,
    )


def run_copies(copies):
    for copy in copies:
        copy.start()
    for copy in copies:
        copy.wait()


def join_kernel(source, out, done):
    pieces, _, wide = source.shape
    run_copies(
        [
            pltpu.make_async_copy(source.at[i], out.at[:, pl.ds(i * wide, wide)], done.at[i])
            for i in range(pieces)
        ]
    )


def join_heads(array):
    pieces, rows, wide = array.shape
    return call(
        join_kernel,
        pltpu.HBM((rows, pieces * wide), array.dtype),
        0,
        4 * rows * pieces * wide,
        in_specs=[VMEM],
        out_specs=HBM,
        scratch_shapes=[pltpu.SemaphoreType.DMA((pieces,))],
    )(array)


def spread(ref, source, count, groups, pitch):
    for group in range(groups):
        ref[pl.ds(group, count, stride=pitch), :] = source[:, group * HD : (group + 1) * HD]


def first_kernel(groups, pitch, *refs):
    gate_far, value_far, rates_far, weights_far, skip_far, query_far, key_far = refs[:7]
    kept, summary, spread_rates, gain, direct, pair = refs[7:13]
    gated, gate, value, rates, weights, skip, query, key, held = refs[13:22]
    small, large, staged, moved, keep = refs[22:]
    rows = gate.shape[0]
    poles = rates.shape[0]
    parts = gate.shape[1] // large.shape[1]
    pieces, _, wide = pair.shape
    parameters = [
        pltpu.make_async_copy(source, target, small.at[i])
        for i, (source, target) in enumerate(
            [(rates_far, rates), (weights_far, weights), (skip_far, skip)]
        )
    ]
    streams = []
    for i in range(large.shape[1]):
        cols = pl.ds(i * parts, parts)
        for which, (source, target) in enumerate([(gate_far, gate), (value_far, value)]):
            streams.append(
                pltpu.make_async_copy(source.at[:, cols], target.at[:, cols], large.at[which, i])
            )
    splits = []
    for which, (source, middle) in enumerate([(query_far, query), (key_far, key)]):
        at = pl.ds(which * rows, rows)
        stage = pltpu.make_async_copy(source, middle, staged.at[which])
        move = pltpu.make_async_copy(held.at[:, at], pair.at[:, at], moved.at[which])
        splits.append((stage, middle, which * rows, move))
    for copy in parameters + [splits[0][0]] + streams + [splits[1][0]]:
        copy.start()
    if pitch != groups:
        for ref in (gated, spread_rates, gain, direct):
            ref[...] = jnp.zeros_like(ref)
    for stage, middle, row, move in splits[:1]:
        stage.wait()
        for i in range(pieces):
            held[i, row : row + rows, :] = middle[:, i * wide : (i + 1) * wide]
        move.start()
    for copy in parameters:
        copy.wait()
    spread(spread_rates, rates[...], poles, groups, pitch)
    spread(gain, weights[...] * jnp.sqrt(rates[...]), poles, groups, pitch)
    spread(direct, skip[...], 1, groups, pitch)
    for group in range(groups):
        if group * HD % parts == 0:
            for copy in streams[2 * (group * HD // parts) :][:2]:
                copy.wait()
        cols = slice(group * HD, (group + 1) * HD)
        product = gate[:, cols].astype(jnp.float32) * value[:, cols].astype(jnp.float32)
        gated[pl.ds(group, rows, stride=pitch), :] = product
    keeping = pltpu.make_async_copy(gated, kept, keep)
    keeping.start()
    for stage, middle, row, move in splits[1:]:
        stage.wait()
        for i in range(pieces):
            held[i, row : row + rows, :] = middle[:, i * wide : (i + 1) * wide]
        move.start()

    slots = [slice(m * pitch, (m + 1) * pitch) for m in range(poles)]
    fades = [jnp.exp(-spread_rates[slot, :]) for slot in slots]

    def one(t, states):
        now = gated[pl.ds(pl.multiple_of(t * pitch, pitch), pitch), :]
        return [fade * state + now for fade, state in zip(fades, states)]

    zero = jnp.zeros((pitch, HD), jnp.float32)
    states = lax.fori_loop(0, rows, one, [zero] * poles, unroll=8)
    for slot, state in zip(slots, states):
        summary[slot, :] = state
    for stage, middle, row, move in splits:
        move.wait()
    keeping.wait()


def first(gate, value, rates, weights, skip, query, key, pitch):
    rows, width = gate.shape
    poles = rates.shape[0]
    heads = width // HD
    streams = 2 if heads % 2 == 0 else 1
    f32 = jnp.float32
    return call(
        functools.partial(first_kernel, heads, pitch),
        (
            pltpu.HBM((rows * pitch, HD), f32),
            jax.ShapeDtypeStruct((poles * pitch, HD), f32),
            jax.ShapeDtypeStruct((poles * pitch, HD), f32),
            jax.ShapeDtypeStruct((poles * pitch, HD), f32),
            jax.ShapeDtypeStruct((pitch, HD), f32),
            pltpu.HBM((heads, 2 * rows, HD), key.dtype),
        ),
        2 * poles * rows * width,
        16 * rows * width,
        in_specs=[HBM] * 7,
        out_specs=(HBM, VMEM, VMEM, VMEM, VMEM, HBM),
        scratch_shapes=[
            pltpu.VMEM((rows * pitch, HD), f32),
            pltpu.VMEM((rows, width), gate.dtype),
            pltpu.VMEM((rows, width), value.dtype),
            pltpu.VMEM(rates.shape, f32),
            pltpu.VMEM(weights.shape, f32),
            pltpu.VMEM(skip.shape, f32),
            pltpu.VMEM((rows, width), query.dtype),
            pltpu.VMEM((rows, width), key.dtype),
            pltpu.VMEM((heads, 2 * rows, HD), key.dtype),
            pltpu.SemaphoreType.DMA((3,)),
            pltpu.SemaphoreType.DMA((2, streams)),
            pltpu.SemaphoreType.DMA((2,)),
            pltpu.SemaphoreType.DMA((2,)),
            pltpu.SemaphoreType.DMA,
        ],
    )(*map(far, (gate, value, rates, weights, skip, query, key)))


def tail_kernel(groups, pitch, kept, carry, rates, gain, direct, gate_far, *refs):
    out, squares, gated, full, gate, come, done = refs
    rows = gate.shape[0]
    runs = come.shape[0]
    run = rows // runs
    streams = []
    for i in range(runs):
        at = pl.ds(i * run * pitch, run * pitch)
        streams.append(pltpu.make_async_copy(kept.at[at], gated.at[at], come.at[i]))
        streams[-1].start()
    fetch = pltpu.make_async_copy(gate_far, gate, done)
    fetch.start()
    slots = [slice(first, first + pitch) for first in range(0, rates.shape[0], pitch)]
    fades = [jnp.exp(-rates[slot, :]) for slot in slots]
    gains = [gain[slot, :] for slot in slots]
    own = direct[...]

    def one(t, states):
        at = pl.ds(pl.multiple_of(t * pitch, pitch), pitch)
        now = gated[at, :]
        states = [fade * state + now for fade, state in zip(fades, states)]
        terms = [own * now] + [g * state for g, state in zip(gains, states)]
        while len(terms) > 1:
            terms = [a + b for a, b in zip(terms[::2], terms[1::2])] + terms[len(terms) // 2 * 2 :]
        full[at, :] = terms[0]
        return states

    states = [carry[slot, :] for slot in slots]
    for i, stream in enumerate(streams):
        stream.wait()
        states = lax.fori_loop(i * run, (i + 1) * run, one, states, unroll=4)
    fetch.wait()
    total = jnp.zeros((rows, HD), jnp.float32)
    for group in range(groups):
        cols = slice(group * HD, (group + 1) * HD)
        conv = gate[:, cols].astype(jnp.float32) * full[pl.ds(group, rows, stride=pitch), :]
        out[group] = conv
        total = total + conv * conv
    ones = jnp.ones((8, HD), jnp.float32)
    summed = lax.dot_general(
        ones,
        total,
        (((1,), (1,)), ((), ())),
        precision=lax.Precision.HIGHEST,
        preferred_element_type=jnp.float32,
    )
    squares[...] = summed[0:1, :]


def tail(gated, carry, rates, gain, direct, gate, pitch):
    rows, width = gate.shape
    poles = rates.shape[0] // pitch
    f32 = jnp.float32
    return call(
        functools.partial(tail_kernel, width // HD, pitch),
        (
            jax.ShapeDtypeStruct((width // HD, rows, HD), f32),
            jax.ShapeDtypeStruct((1, rows), f32),
        ),
        3000 * poles * rows * width,
        10 * rows * width,
        in_specs=[HBM] + [VMEM] * 4 + [HBM],
        scratch_shapes=[
            pltpu.VMEM((rows * pitch, HD), f32),
            pltpu.VMEM((rows * pitch, HD), f32),
            pltpu.VMEM((rows, width), gate.dtype),
            pltpu.SemaphoreType.DMA((4 if rows % 32 == 0 else 1,)),
            pltpu.SemaphoreType.DMA,
        ],
    )(far(gated), carry, rates, gain, direct, far(gate))


def places(runs):
    index = lax.axis_index("seq")
    return index // PLANE % runs, index % PLANE


def norm_kernel(channels, conv, squares, *outs):
    runs, rows, _ = outs[0].shape
    run, place = places(runs)
    scale = lax.rsqrt(squares[...] / channels + 1e-06)
    scale = jnp.transpose(jnp.broadcast_to(scale, (HD, rows)))
    for j in range(PLANE):
        for k in range(runs):
            outs[j][k] = (conv[(run ^ k) * PLANE + (place ^ j)] * scale).astype(outs[j].dtype)


def normalize(conv, squares, channels):
    heads, rows, _ = conv.shape
    message = jax.ShapeDtypeStruct((heads // PLANE, rows, HD), jnp.bfloat16)
    return call(
        functools.partial(norm_kernel, channels),
        (message,) * PLANE,
        heads * rows * HD,
        6 * heads * rows * HD,
    )(conv, squares)


def prefix_state(summary, rates, block_rows, axis):
    size = lax.axis_size(axis)
    place = lax.axis_index(axis)
    span = rates * jnp.float32(block_rows)

    def fade(blocks):
        return jnp.exp(-span * jnp.maximum(blocks, 0).astype(jnp.float32))

    strides = [1]
    while strides[-1] * 4 < size:
        strides.append(strides[-1] * 4)
    before, above = None, size
    for stride in reversed(strides):
        many = above // stride
        digit, inside = place // stride % many, place % above
        total = None if before is None else fade(digit * stride) * before
        for k in range(1, many):
            other = digit ^ k
            gap = other * stride - inside - 1
            sent = summary
            if before is not None:
                sent = fade(other * stride) * before + jnp.where(
                    digit < other, fade(gap) * summary, 0.0
                )
            got = lax.ppermute(sent, axis, [(i, i ^ (stride * k)) for i in range(size)])
            if before is None:
                gap = digit * stride - (inside - digit * stride + other * stride) - 1
                got = jnp.where(other < digit, fade(gap) * got, 0.0)
            total = got if total is None else total + got
        before, above = total, stride
    return before


def attend_kernel(block, pair, *refs):
    *parts, out, scores, values = refs
    _, runs, twice, _ = pair.shape
    rows = twice // 2
    per_block = block // rows
    turns = runs * PLANE // per_block
    own_run, own_place = places(runs)
    factor = LOG2E * HD ** (-0.5)
    row = lax.broadcasted_iota(jnp.int32, (block, block), 0)
    col = lax.broadcasted_iota(jnp.int32, (block, block), 1)
    visible = col <= row
    for k, part in enumerate(parts):
        for j in range(PLANE):
            values[own_run ^ k, own_place ^ j] = part[j]

    def piece(turn, first):
        run, inside = divmod(turn * per_block, PLANE)
        got = [pair[inside + i, run, first : first + rows, :] for i in range(per_block)]
        return jnp.concatenate(got, axis=0)

    def score(turn, part, top):
        got = lax.dot_general(
            piece(turn, 0),
            piece(part, rows),
            (((1,), (1,)), ((), ())),
            preferred_element_type=jnp.float32,
        )
        if part == turn:
            got = jnp.where(visible, got, -1e30)
        scores[turn % 2, :, part * block : (part + 1) * block] = got
        for lane in range(0, block, HD):
            one = got[:, lane : lane + HD]
            top = one if top is None else jnp.maximum(top, one)
        return top

    def weigh(turn, part, top, total, mixed):
        got = scores[turn % 2, :, part * block : (part + 1) * block]
        expo = jnp.exp2(got * factor - top)
        for lane in range(0, block, HD):
            total = total + expo[:, lane : lane + HD]
        run, inside = divmod(part * per_block, PLANE)
        value = values[run, inside : inside + per_block].reshape(block, HD)
        mixed = mixed + jnp.dot(
            expo.astype(jnp.bfloat16), value, preferred_element_type=jnp.float32
        )
        return total, mixed

    zero = jnp.zeros((block, HD), jnp.float32)
    top = score(0, 0, None)
    for turn in range(turns):
        peak = jnp.max(top, axis=1, keepdims=True) * factor
        top, total, mixed = None, zero, zero
        for part in range(turn + 2):
            if turn + 1 < turns:
                top = score(turn + 1, part, top)
            if part <= turn:
                total, mixed = weigh(turn, part, peak, total, mixed)
        mixed = mixed / jnp.sum(total, axis=1, keepdims=True)
        out[turn * per_block : (turn + 1) * per_block] = mixed.astype(out.dtype).reshape(
            per_block, rows, HD
        )


def attend(pair, parts):
    _, runs, twice, _ = pair.shape
    rows = twice // 2
    block = rows
    while block < 256 and PLANE * rows % (2 * block) == 0:
        block *= 2
    length = runs * PLANE * rows
    return call(
        functools.partial(attend_kernel, block),
        jax.ShapeDtypeStruct((runs * PLANE, rows, HD), jnp.bfloat16),
        2 * length * length * HD,
        8 * length * HD,
        length * length // 2,
        scratch_shapes=[
            pltpu.VMEM((2, block, length), jnp.float32),
            pltpu.VMEM((runs, PLANE, rows, HD), jnp.bfloat16),
        ],
    )(pair, *parts)


def gathered_head(query, key, value, first_row):
    count, step = key.shape[0], math.gcd(key.shape[0], 1024)
    query_pos = first_row + jnp.arange(query.shape[0], dtype=jnp.int32)

    def one(turn, carried):
        top, total, mixed = carried
        keys = lax.dynamic_slice_in_dim(key, turn * step, step, 0)
        values = lax.dynamic_slice_in_dim(value, turn * step, step, 0)
        scores = jnp.dot(query, keys.T, preferred_element_type=jnp.float32) * HD ** (-0.5)
        visible = (turn * step + jnp.arange(step, dtype=jnp.int32))[None, :] <= query_pos[:, None]
        scores = jnp.where(visible, scores, -1e30)
        new_top = jnp.maximum(top, jnp.max(scores, axis=1, keepdims=True))
        rescale = jnp.exp(top - new_top)
        expo = jnp.where(visible, jnp.exp(scores - new_top), 0.0)
        total = total * rescale + jnp.sum(expo, axis=1, keepdims=True)
        part = jnp.dot(expo.astype(jnp.bfloat16), values, preferred_element_type=jnp.float32)
        return new_top, total, mixed * rescale + part

    rows = query.shape[0]
    start = (
        jnp.full((rows, 1), -1e30, jnp.float32),
        jnp.zeros((rows, 1), jnp.float32),
        jnp.zeros((rows, HD), jnp.float32),
    )
    _, total, mixed = lax.fori_loop(0, count // step, one, start)
    return (mixed / total).astype(jnp.bfloat16)


def local(
    gate_outer, gate_inner, value_in, pole_rates, pole_weights, skip_gain, query_rows, key_rows
):
    rows, width = gate_outer.shape
    heads = width // HD
    size = lax.axis_size("seq")
    channels = width * lax.axis_size("chan")
    group_count = size // heads
    runs = heads // PLANE
    pitch = -(-heads // 8) * 8

    def exchange(array, members, stride=1):
        if members == 1:
            return array
        span = members * stride
        teams = [
            list(range(first + offset, first + span, stride))
            for first in range(0, size, span)
            for offset in range(stride)
        ]
        return lax.all_to_all(
            array, "seq", 0, 0, axis_index_groups=teams if members < size else None
        )

    def swap(array, distance):
        if distance == 0:
            return array
        return lax.ppermute(array, "seq", [(i, i ^ distance) for i in range(size)])

    gated, summary, rates, gain, direct, chunks = first(
        gate_inner, value_in, pole_rates, pole_weights, skip_gain[None, :], query_rows, key_rows, pitch
    )
    pair = exchange(chunks.reshape(runs, PLANE, 2 * rows, HD), runs, PLANE)
    carry = prefix_state(summary, rates, rows, "seq")
    conv, squares = tail(gated, carry, rates, gain, direct, gate_outer, pitch)
    messages = normalize(conv, lax.psum(squares, "chan"), channels)
    near = [swap(message, j) for j, message in enumerate(messages)]
    values = [swap(jnp.stack([part[k] for part in near]), k * PLANE) for k in range(runs)]
    pair = exchange(jnp.swapaxes(pair, 0, 1), PLANE)
    if group_count == 1:
        mixed = attend(pair, values)
    else:
        mine = lax.axis_index("seq") // heads
        others = [list(range(h, size, heads)) for h in range(heads)]
        gather = functools.partial(
            lax.all_gather, axis_name="seq", axis_index_groups=others, tiled=True
        )
        span = heads * rows
        run, place = places(runs)
        values = [
            jnp.stack(values)[run ^ (h // PLANE), place ^ (h % PLANE)] for h in range(heads)
        ]
        pair = jnp.swapaxes(pair, 0, 1)
        mixed = gathered_head(
            pair[:, :, :rows].reshape(span, HD),
            gather(pair[:, :, rows:].reshape(span, HD)),
            gather(jnp.concatenate(values)),
            mine * span,
        ).reshape(heads, rows, HD)
    return join_heads(exchange(mixed, heads))


def solution(mesh):
    rows = P("seq", "chan")
    poles = P(None, "chan")
    return jax.shard_map(
        local,
        mesh=mesh,
        in_specs=(rows, rows, rows, poles, poles, P("chan"), rows, rows),
        out_specs=rows,
        check_vma=False,
    )
```

```python
import functools
import math

import jax
import jax.numpy as jnp
from jax import lax
from jax.experimental import pallas as pl
from jax.experimental.pallas import tpu as pltpu
from jax.sharding import PartitionSpec as P

HD = 128
LOG2E = math.log2(math.e)
PLANE = 4
HBM = pl.BlockSpec(memory_space=pltpu.HBM)
VMEM = pl.BlockSpec(memory_space=pltpu.VMEM)


def far(array):
    return pltpu.with_memory_space_constraint(array, pltpu.HBM)


def near(array):
    return pltpu.with_memory_space_constraint(array, pltpu.VMEM)
VMEM_CAP = 12 * 1024 * 1024


def call(body, out_shape, flops, moved, exps=0, **kwargs):
    return pl.pallas_call(
        body,
        out_shape=out_shape,
        compiler_params=pltpu.CompilerParams(vmem_limit_bytes=VMEM_CAP),
        cost_estimate=pl.CostEstimate(flops=flops, bytes_accessed=moved, transcendentals=exps),
        **kwargs,
    )


def run_copies(copies):
    for copy in copies:
        copy.start()
    for copy in copies:
        copy.wait()


def join_kernel(source, out, done):
    pieces, _, wide = source.shape
    run_copies(
        [
            pltpu.make_async_copy(source.at[i], out.at[:, pl.ds(i * wide, wide)], done.at[i])
            for i in range(pieces)
        ]
    )


def join_heads(array):
    pieces, rows, wide = array.shape
    return call(
        join_kernel,
        pltpu.HBM((rows, pieces * wide), array.dtype),
        0,
        4 * rows * pieces * wide,
        in_specs=[VMEM],
        out_specs=HBM,
        scratch_shapes=[pltpu.SemaphoreType.DMA((pieces,))],
    )(array)


def spread(ref, source, count, groups, pitch):
    for group in range(groups):
        ref[pl.ds(group, count, stride=pitch), :] = source[:, group * HD : (group + 1) * HD]


def first_kernel(groups, pitch, *refs):
    gate_far, value_far, rates_far, weights_far, skip_far, query_far, key_far = refs[:7]
    kept, summary, spread_rates, gain, direct, pair = refs[7:13]
    gated, gate, value, rates, weights, skip, query, key, held = refs[13:22]
    small, large, staged, moved, keep = refs[22:]
    rows = gate.shape[0]
    poles = rates.shape[0]
    parts = gate.shape[1] // large.shape[1]
    pieces, _, wide = pair.shape
    parameters = [
        pltpu.make_async_copy(source, target, small.at[i])
        for i, (source, target) in enumerate(
            [(rates_far, rates), (weights_far, weights), (skip_far, skip)]
        )
    ]
    streams = []
    for i in range(large.shape[1]):
        cols = pl.ds(i * parts, parts)
        for which, (source, target) in enumerate([(gate_far, gate), (value_far, value)]):
            streams.append(
                pltpu.make_async_copy(source.at[:, cols], target.at[:, cols], large.at[which, i])
            )
    splits = []
    for which, (source, middle) in enumerate([(query_far, query), (key_far, key)]):
        at = pl.ds(which * rows, rows)
        stage = pltpu.make_async_copy(source, middle, staged.at[which])
        move = pltpu.make_async_copy(held.at[:, at], pair.at[:, at], moved.at[which])
        splits.append((stage, middle, which * rows, move))
    for copy in parameters + [splits[0][0]] + streams + [splits[1][0]]:
        copy.start()
    if pitch != groups:
        for ref in (gated, spread_rates, gain, direct):
            ref[...] = jnp.zeros_like(ref)
    for stage, middle, row, move in splits[:1]:
        stage.wait()
        for i in range(pieces):
            held[i, row : row + rows, :] = middle[:, i * wide : (i + 1) * wide]
        move.start()
    for copy in parameters:
        copy.wait()
    spread(spread_rates, rates[...], poles, groups, pitch)
    spread(gain, weights[...] * jnp.sqrt(rates[...]), poles, groups, pitch)
    spread(direct, skip[...], 1, groups, pitch)
    for group in range(groups):
        if group * HD % parts == 0:
            for copy in streams[2 * (group * HD // parts) :][:2]:
                copy.wait()
        cols = slice(group * HD, (group + 1) * HD)
        product = gate[:, cols].astype(jnp.float32) * value[:, cols].astype(jnp.float32)
        gated[pl.ds(group, rows, stride=pitch), :] = product
    keeping = pltpu.make_async_copy(gated, kept, keep)
    keeping.start()
    for stage, middle, row, move in splits[1:]:
        stage.wait()
        for i in range(pieces):
            held[i, row : row + rows, :] = middle[:, i * wide : (i + 1) * wide]
        move.start()

    slots = [slice(m * pitch, (m + 1) * pitch) for m in range(poles)]
    fades = [jnp.exp(-spread_rates[slot, :]) for slot in slots]

    def one(t, states):
        now = gated[pl.ds(pl.multiple_of(t * pitch, pitch), pitch), :]
        return [fade * state + now for fade, state in zip(fades, states)]

    zero = jnp.zeros((pitch, HD), jnp.float32)
    states = lax.fori_loop(0, rows, one, [zero] * poles, unroll=8)
    for slot, state in zip(slots, states):
        summary[slot, :] = state
    for stage, middle, row, move in splits:
        move.wait()
    keeping.wait()


def first(gate, value, rates, weights, skip, query, key, pitch):
    rows, width = gate.shape
    poles = rates.shape[0]
    heads = width // HD
    streams = 2 if heads % 2 == 0 else 1
    f32 = jnp.float32
    return call(
        functools.partial(first_kernel, heads, pitch),
        (
            pltpu.HBM((rows * pitch, HD), f32),
            jax.ShapeDtypeStruct((poles * pitch, HD), f32),
            jax.ShapeDtypeStruct((poles * pitch, HD), f32),
            jax.ShapeDtypeStruct((poles * pitch, HD), f32),
            jax.ShapeDtypeStruct((pitch, HD), f32),
            pltpu.HBM((heads, 2 * rows, HD), key.dtype),
        ),
        2 * poles * rows * width,
        16 * rows * width,
        in_specs=[HBM] * 7,
        out_specs=(HBM, VMEM, VMEM, VMEM, VMEM, HBM),
        scratch_shapes=[
            pltpu.VMEM((rows * pitch, HD), f32),
            pltpu.VMEM((rows, width), gate.dtype),
            pltpu.VMEM((rows, width), value.dtype),
            pltpu.VMEM(rates.shape, f32),
            pltpu.VMEM(weights.shape, f32),
            pltpu.VMEM(skip.shape, f32),
            pltpu.VMEM((rows, width), query.dtype),
            pltpu.VMEM((rows, width), key.dtype),
            pltpu.VMEM((heads, 2 * rows, HD), key.dtype),
            pltpu.SemaphoreType.DMA((3,)),
            pltpu.SemaphoreType.DMA((2, streams)),
            pltpu.SemaphoreType.DMA((2,)),
            pltpu.SemaphoreType.DMA((2,)),
            pltpu.SemaphoreType.DMA,
        ],
    )(*map(far, (gate, value, rates, weights, skip, query, key)))


def tail_kernel(groups, pitch, kept, carry, rates, gain, direct, gate_far, *refs):
    out, squares, gated, full, gate, come, done = refs
    rows = gate.shape[0]
    runs = come.shape[0]
    run = rows // runs
    streams = []
    for i in range(runs):
        at = pl.ds(i * run * pitch, run * pitch)
        streams.append(pltpu.make_async_copy(kept.at[at], gated.at[at], come.at[i]))
        streams[-1].start()
    fetch = pltpu.make_async_copy(gate_far, gate, done)
    fetch.start()
    slots = [slice(first, first + pitch) for first in range(0, rates.shape[0], pitch)]
    fades = [jnp.exp(-rates[slot, :]) for slot in slots]
    gains = [gain[slot, :] for slot in slots]
    own = direct[...]

    def one(t, states):
        at = pl.ds(pl.multiple_of(t * pitch, pitch), pitch)
        now = gated[at, :]
        states = [fade * state + now for fade, state in zip(fades, states)]
        terms = [own * now] + [g * state for g, state in zip(gains, states)]
        while len(terms) > 1:
            terms = [a + b for a, b in zip(terms[::2], terms[1::2])] + terms[len(terms) // 2 * 2 :]
        full[at, :] = terms[0]
        return states

    states = [carry[slot, :] for slot in slots]
    for i, stream in enumerate(streams):
        stream.wait()
        states = lax.fori_loop(i * run, (i + 1) * run, one, states, unroll=4)
    fetch.wait()
    total = jnp.zeros((rows, HD), jnp.float32)
    for group in range(groups):
        cols = slice(group * HD, (group + 1) * HD)
        conv = gate[:, cols].astype(jnp.float32) * full[pl.ds(group, rows, stride=pitch), :]
        out[group] = conv
        total = total + conv * conv
    ones = jnp.ones((8, HD), jnp.float32)
    summed = lax.dot_general(
        ones,
        total,
        (((1,), (1,)), ((), ())),
        precision=lax.Precision.HIGHEST,
        preferred_element_type=jnp.float32,
    )
    squares[...] = summed[0:1, :]


def tail(gated, carry, rates, gain, direct, gate, pitch):
    rows, width = gate.shape
    poles = rates.shape[0] // pitch
    f32 = jnp.float32
    return call(
        functools.partial(tail_kernel, width // HD, pitch),
        (
            jax.ShapeDtypeStruct((width // HD, rows, HD), f32),
            jax.ShapeDtypeStruct((1, rows), f32),
        ),
        3000 * poles * rows * width,
        10 * rows * width,
        in_specs=[HBM] + [VMEM] * 4 + [HBM],
        scratch_shapes=[
            pltpu.VMEM((rows * pitch, HD), f32),
            pltpu.VMEM((rows * pitch, HD), f32),
            pltpu.VMEM((rows, width), gate.dtype),
            pltpu.SemaphoreType.DMA((4 if rows % 32 == 0 else 1,)),
            pltpu.SemaphoreType.DMA,
        ],
    )(far(gated), carry, rates, gain, direct, far(gate))


def places(runs):
    index = lax.axis_index("seq")
    return index // PLANE % runs, index % PLANE


def norm_kernel(channels, conv, squares, *outs):
    runs, rows, _ = outs[0].shape
    run, place = places(runs)
    scale = lax.rsqrt(squares[...] / channels + 1e-06)
    scale = jnp.transpose(jnp.broadcast_to(scale, (HD, rows)))
    for j in range(PLANE):
        for k in range(runs):
            outs[j][k] = (conv[(run ^ k) * PLANE + (place ^ j)] * scale).astype(outs[j].dtype)


def normalize(conv, squares, channels):
    heads, rows, _ = conv.shape
    message = jax.ShapeDtypeStruct((heads // PLANE, rows, HD), jnp.bfloat16)
    return call(
        functools.partial(norm_kernel, channels),
        (message,) * PLANE,
        heads * rows * HD,
        6 * heads * rows * HD,
    )(conv, squares)


def prefix_state(summary, rates, block_rows, axis):
    size = lax.axis_size(axis)
    place = lax.axis_index(axis)
    span = rates * jnp.float32(block_rows)

    def fade(blocks):
        return jnp.exp(-span * jnp.maximum(blocks, 0).astype(jnp.float32))

    strides = [1]
    while strides[-1] * 4 < size:
        strides.append(strides[-1] * 4)
    before, above = None, size
    for stride in reversed(strides):
        many = above // stride
        digit, inside = place // stride % many, place % above
        total = None if before is None else fade(digit * stride) * before
        for k in range(1, many):
            other = digit ^ k
            gap = other * stride - inside - 1
            sent = summary
            if before is not None:
                sent = fade(other * stride) * before + jnp.where(
                    digit < other, fade(gap) * summary, 0.0
                )
            got = lax.ppermute(sent, axis, [(i, i ^ (stride * k)) for i in range(size)])
            if before is None:
                gap = digit * stride - (inside - digit * stride + other * stride) - 1
                got = jnp.where(other < digit, fade(gap) * got, 0.0)
            total = got if total is None else total + got
        before, above = total, stride
    return before


def attend_kernel(block, pair, *refs):
    *parts, out, scores, values = refs
    _, runs, twice, _ = pair.shape
    rows = twice // 2
    per_block = block // rows
    turns = runs * PLANE // per_block
    own_run, own_place = places(runs)
    factor = LOG2E * HD ** (-0.5)
    row = lax.broadcasted_iota(jnp.int32, (block, block), 0)
    col = lax.broadcasted_iota(jnp.int32, (block, block), 1)
    visible = col <= row
    for k, part in enumerate(parts):
        for j in range(PLANE):
            values[own_run ^ k, own_place ^ j] = part[j]

    def piece(turn, first):
        run, inside = divmod(turn * per_block, PLANE)
        got = [pair[inside + i, run, first : first + rows, :] for i in range(per_block)]
        return jnp.concatenate(got, axis=0)

    def score(turn, part, top):
        got = lax.dot_general(
            piece(turn, 0),
            piece(part, rows),
            (((1,), (1,)), ((), ())),
            preferred_element_type=jnp.float32,
        )
        if part == turn:
            got = jnp.where(visible, got, -1e30)
        scores[turn % 2, :, part * block : (part + 1) * block] = got
        for lane in range(0, block, HD):
            one = got[:, lane : lane + HD]
            top = one if top is None else jnp.maximum(top, one)
        return top

    def weigh(turn, part, top, total, mixed):
        got = scores[turn % 2, :, part * block : (part + 1) * block]
        expo = jnp.exp2(got * factor - top)
        for lane in range(0, block, HD):
            total = total + expo[:, lane : lane + HD]
        run, inside = divmod(part * per_block, PLANE)
        value = values[run, inside : inside + per_block].reshape(block, HD)
        mixed = mixed + jnp.dot(
            expo.astype(jnp.bfloat16), value, preferred_element_type=jnp.float32
        )
        return total, mixed

    zero = jnp.zeros((block, HD), jnp.float32)
    top = score(0, 0, None)
    for turn in range(turns):
        peak = jnp.max(top, axis=1, keepdims=True) * factor
        top, total, mixed = None, zero, zero
        for part in range(turn + 2):
            if turn + 1 < turns:
                top = score(turn + 1, part, top)
            if part <= turn:
                total, mixed = weigh(turn, part, peak, total, mixed)
        mixed = mixed / jnp.sum(total, axis=1, keepdims=True)
        out[turn * per_block : (turn + 1) * per_block] = mixed.astype(out.dtype).reshape(
            per_block, rows, HD
        )


def attend(pair, parts):
    _, runs, twice, _ = pair.shape
    rows = twice // 2
    block = rows
    while block < 256 and PLANE * rows % (2 * block) == 0:
        block *= 2
    length = runs * PLANE * rows
    return call(
        functools.partial(attend_kernel, block),
        jax.ShapeDtypeStruct((runs * PLANE, rows, HD), jnp.bfloat16),
        2 * length * length * HD,
        8 * length * HD,
        length * length // 2,
        scratch_shapes=[
            pltpu.VMEM((2, block, length), jnp.float32),
            pltpu.VMEM((runs, PLANE, rows, HD), jnp.bfloat16),
        ],
    )(pair, *parts)


def gathered_head(query, key, value, first_row):
    count, step = key.shape[0], math.gcd(key.shape[0], 1024)
    query_pos = first_row + jnp.arange(query.shape[0], dtype=jnp.int32)

    def one(turn, carried):
        top, total, mixed = carried
        keys = lax.dynamic_slice_in_dim(key, turn * step, step, 0)
        values = lax.dynamic_slice_in_dim(value, turn * step, step, 0)
        scores = jnp.dot(query, keys.T, preferred_element_type=jnp.float32) * HD ** (-0.5)
        visible = (turn * step + jnp.arange(step, dtype=jnp.int32))[None, :] <= query_pos[:, None]
        scores = jnp.where(visible, scores, -1e30)
        new_top = jnp.maximum(top, jnp.max(scores, axis=1, keepdims=True))
        rescale = jnp.exp(top - new_top)
        expo = jnp.where(visible, jnp.exp(scores - new_top), 0.0)
        total = total * rescale + jnp.sum(expo, axis=1, keepdims=True)
        part = jnp.dot(expo.astype(jnp.bfloat16), values, preferred_element_type=jnp.float32)
        return new_top, total, mixed * rescale + part

    rows = query.shape[0]
    start = (
        jnp.full((rows, 1), -1e30, jnp.float32),
        jnp.zeros((rows, 1), jnp.float32),
        jnp.zeros((rows, HD), jnp.float32),
    )
    _, total, mixed = lax.fori_loop(0, count // step, one, start)
    return (mixed / total).astype(jnp.bfloat16)


def local(
    gate_outer, gate_inner, value_in, pole_rates, pole_weights, skip_gain, query_rows, key_rows
):
    rows, width = gate_outer.shape
    heads = width // HD
    size = lax.axis_size("seq")
    channels = width * lax.axis_size("chan")
    group_count = size // heads
    runs = heads // PLANE
    pitch = -(-heads // 8) * 8

    def exchange(array, members, stride=1):
        if members == 1:
            return array
        span = members * stride
        teams = [
            list(range(first + offset, first + span, stride))
            for first in range(0, size, span)
            for offset in range(stride)
        ]
        return lax.all_to_all(
            array, "seq", 0, 0, axis_index_groups=teams if members < size else None
        )

    def across(array):
        if channels != 2 * width:
            return lax.psum(array, "chan")
        return array + lax.ppermute(array, "chan", [(0, 1), (1, 0)])

    def swap(array, distance):
        if distance == 0:
            return array
        return lax.ppermute(array, "seq", [(i, i ^ distance) for i in range(size)])

    gated, summary, rates, gain, direct, chunks = first(
        gate_inner, value_in, pole_rates, pole_weights, skip_gain[None, :], query_rows, key_rows, pitch
    )
    pair = exchange(chunks.reshape(runs, PLANE, 2 * rows, HD), runs, PLANE)
    carry = prefix_state(summary, rates, rows, "seq")
    conv, squares = tail(gated, carry, rates, gain, direct, gate_outer, pitch)
    messages = normalize(conv, across(squares), channels)
    near = [swap(message, j) for j, message in enumerate(messages)]
    values = [swap(jnp.stack([part[k] for part in near]), k * PLANE) for k in range(runs)]
    pair = exchange(jnp.swapaxes(pair, 0, 1), PLANE)
    if group_count == 1:
        mixed = attend(pair, values)
    else:
        mine = lax.axis_index("seq") // heads
        others = [list(range(h, size, heads)) for h in range(heads)]
        gather = functools.partial(
            lax.all_gather, axis_name="seq", axis_index_groups=others, tiled=True
        )
        span = heads * rows
        run, place = places(runs)
        values = [
            jnp.stack(values)[run ^ (h // PLANE), place ^ (h % PLANE)] for h in range(heads)
        ]
        pair = jnp.swapaxes(pair, 0, 1)
        mixed = gathered_head(
            pair[:, :, :rows].reshape(span, HD),
            gather(pair[:, :, rows:].reshape(span, HD)),
            gather(jnp.concatenate(values)),
            mine * span,
        ).reshape(heads, rows, HD)
    return join_heads(exchange(mixed, heads))


def solution(mesh):
    rows = P("seq", "chan")
    poles = P(None, "chan")
    return jax.shard_map(
        local,
        mesh=mesh,
        in_specs=(rows, rows, rows, poles, poles, P("chan"), rows, rows),
        out_specs=rows,
        check_vma=False,
    )
```

```python
import functools
import math

import jax
import jax.numpy as jnp
from jax import lax
from jax.experimental import pallas as pl
from jax.experimental.pallas import tpu as pltpu
from jax.sharding import PartitionSpec as P

HD = 128
LOG2E = math.log2(math.e)
PLANE = 4
HBM = pl.BlockSpec(memory_space=pltpu.HBM)
VMEM = pl.BlockSpec(memory_space=pltpu.VMEM)


def far(array):
    return pltpu.with_memory_space_constraint(array, pltpu.HBM)


def near(array):
    return pltpu.with_memory_space_constraint(array, pltpu.VMEM)
VMEM_CAP = 20 * 1024 * 1024


def call(body, out_shape, flops, moved, exps=0, **kwargs):
    return pl.pallas_call(
        body,
        out_shape=out_shape,
        compiler_params=pltpu.CompilerParams(vmem_limit_bytes=VMEM_CAP),
        cost_estimate=pl.CostEstimate(flops=flops, bytes_accessed=moved, transcendentals=exps),
        **kwargs,
    )


def run_copies(copies):
    for copy in copies:
        copy.start()
    for copy in copies:
        copy.wait()


def join_kernel(source, out, done):
    pieces, _, wide = source.shape
    run_copies(
        [
            pltpu.make_async_copy(source.at[i], out.at[:, pl.ds(i * wide, wide)], done.at[i])
            for i in range(pieces)
        ]
    )


def join_heads(array):
    pieces, rows, wide = array.shape
    return call(
        join_kernel,
        pltpu.HBM((rows, pieces * wide), array.dtype),
        0,
        4 * rows * pieces * wide,
        in_specs=[VMEM],
        out_specs=HBM,
        scratch_shapes=[pltpu.SemaphoreType.DMA((pieces,))],
    )(array)


def spread(ref, source, count, groups, pitch):
    for group in range(groups):
        ref[pl.ds(group, count, stride=pitch), :] = source[:, group * HD : (group + 1) * HD]


def first_kernel(groups, pitch, *refs):
    gate_far, value_far, rates_far, weights_far, skip_far, query_far, key_far = refs[:7]
    kept, summary, spread_rates, gain, direct, pair = refs[7:13]
    gated, gate, value, rates, weights, skip, query, key, held = refs[13:22]
    small, large, staged, moved, keep = refs[22:]
    rows = gate.shape[0]
    poles = rates.shape[0]
    parts = gate.shape[1] // large.shape[1]
    pieces, _, wide = pair.shape
    parameters = [
        pltpu.make_async_copy(source, target, small.at[i])
        for i, (source, target) in enumerate(
            [(rates_far, rates), (weights_far, weights), (skip_far, skip)]
        )
    ]
    streams = []
    for i in range(large.shape[1]):
        cols = pl.ds(i * parts, parts)
        for which, (source, target) in enumerate([(gate_far, gate), (value_far, value)]):
            streams.append(
                pltpu.make_async_copy(source.at[:, cols], target.at[:, cols], large.at[which, i])
            )
    splits = []
    for which, (source, middle) in enumerate([(query_far, query), (key_far, key)]):
        at = pl.ds(which * rows, rows)
        stage = pltpu.make_async_copy(source, middle, staged.at[which])
        move = pltpu.make_async_copy(held.at[:, at], pair.at[:, at], moved.at[which])
        splits.append((stage, middle, which * rows, move))
    for copy in parameters + [splits[0][0]] + streams + [splits[1][0]]:
        copy.start()
    if pitch != groups:
        for ref in (gated, spread_rates, gain, direct):
            ref[...] = jnp.zeros_like(ref)
    for stage, middle, row, move in splits[:1]:
        stage.wait()
        for i in range(pieces):
            held[i, row : row + rows, :] = middle[:, i * wide : (i + 1) * wide]
        move.start()
    for copy in parameters:
        copy.wait()
    spread(spread_rates, rates[...], poles, groups, pitch)
    spread(gain, weights[...] * jnp.sqrt(rates[...]), poles, groups, pitch)
    spread(direct, skip[...], 1, groups, pitch)
    for group in range(groups):
        if group * HD % parts == 0:
            for copy in streams[2 * (group * HD // parts) :][:2]:
                copy.wait()
        cols = slice(group * HD, (group + 1) * HD)
        product = gate[:, cols].astype(jnp.float32) * value[:, cols].astype(jnp.float32)
        gated[pl.ds(group, rows, stride=pitch), :] = product
    keeping = pltpu.make_async_copy(gated, kept, keep)
    keeping.start()
    for stage, middle, row, move in splits[1:]:
        stage.wait()
        for i in range(pieces):
            held[i, row : row + rows, :] = middle[:, i * wide : (i + 1) * wide]
        move.start()

    slots = [slice(m * pitch, (m + 1) * pitch) for m in range(poles)]
    fades = [jnp.exp(-spread_rates[slot, :]) for slot in slots]

    def one(t, states):
        now = gated[pl.ds(pl.multiple_of(t * pitch, pitch), pitch), :]
        return [fade * state + now for fade, state in zip(fades, states)]

    zero = jnp.zeros((pitch, HD), jnp.float32)
    states = lax.fori_loop(0, rows, one, [zero] * poles, unroll=8)
    for slot, state in zip(slots, states):
        summary[slot, :] = state
    for stage, middle, row, move in splits:
        move.wait()
    keeping.wait()


def first(gate, value, rates, weights, skip, query, key, pitch):
    rows, width = gate.shape
    poles = rates.shape[0]
    heads = width // HD
    streams = 2 if heads % 2 == 0 else 1
    f32 = jnp.float32
    return call(
        functools.partial(first_kernel, heads, pitch),
        (
            pltpu.HBM((rows * pitch, HD), f32),
            jax.ShapeDtypeStruct((poles * pitch, HD), f32),
            jax.ShapeDtypeStruct((poles * pitch, HD), f32),
            jax.ShapeDtypeStruct((poles * pitch, HD), f32),
            jax.ShapeDtypeStruct((pitch, HD), f32),
            pltpu.HBM((heads, 2 * rows, HD), key.dtype),
        ),
        2 * poles * rows * width,
        16 * rows * width,
        in_specs=[HBM] * 7,
        out_specs=(HBM, VMEM, VMEM, VMEM, VMEM, HBM),
        scratch_shapes=[
            pltpu.VMEM((rows * pitch, HD), f32),
            pltpu.VMEM((rows, width), gate.dtype),
            pltpu.VMEM((rows, width), value.dtype),
            pltpu.VMEM(rates.shape, f32),
            pltpu.VMEM(weights.shape, f32),
            pltpu.VMEM(skip.shape, f32),
            pltpu.VMEM((rows, width), query.dtype),
            pltpu.VMEM((rows, width), key.dtype),
            pltpu.VMEM((heads, 2 * rows, HD), key.dtype),
            pltpu.SemaphoreType.DMA((3,)),
            pltpu.SemaphoreType.DMA((2, streams)),
            pltpu.SemaphoreType.DMA((2,)),
            pltpu.SemaphoreType.DMA((2,)),
            pltpu.SemaphoreType.DMA,
        ],
    )(*map(far, (gate, value, rates, weights, skip, query, key)))


def tail_kernel(groups, pitch, kept, carry, rates, gain, direct, gate_far, *refs):
    out, squares, gated, full, gate, come, done = refs
    rows = gate.shape[0]
    runs = come.shape[0]
    run = rows // runs
    streams = []
    for i in range(runs):
        at = pl.ds(i * run * pitch, run * pitch)
        streams.append(pltpu.make_async_copy(kept.at[at], gated.at[at], come.at[i]))
        streams[-1].start()
    fetch = pltpu.make_async_copy(gate_far, gate, done)
    fetch.start()
    slots = [slice(first, first + pitch) for first in range(0, rates.shape[0], pitch)]
    fades = [jnp.exp(-rates[slot, :]) for slot in slots]
    gains = [gain[slot, :] for slot in slots]
    own = direct[...]

    def one(t, states):
        at = pl.ds(pl.multiple_of(t * pitch, pitch), pitch)
        now = gated[at, :]
        states = [fade * state + now for fade, state in zip(fades, states)]
        terms = [own * now] + [g * state for g, state in zip(gains, states)]
        while len(terms) > 1:
            terms = [a + b for a, b in zip(terms[::2], terms[1::2])] + terms[len(terms) // 2 * 2 :]
        full[at, :] = terms[0]
        return states

    states = [carry[slot, :] for slot in slots]
    for i, stream in enumerate(streams):
        stream.wait()
        states = lax.fori_loop(i * run, (i + 1) * run, one, states, unroll=4)
    fetch.wait()
    total = jnp.zeros((rows, HD), jnp.float32)
    for group in range(groups):
        cols = slice(group * HD, (group + 1) * HD)
        conv = gate[:, cols].astype(jnp.float32) * full[pl.ds(group, rows, stride=pitch), :]
        out[group] = conv
        total = total + conv * conv
    ones = jnp.ones((8, HD), jnp.float32)
    summed = lax.dot_general(
        ones,
        total,
        (((1,), (1,)), ((), ())),
        precision=lax.Precision.HIGHEST,
        preferred_element_type=jnp.float32,
    )
    squares[...] = summed[0:1, :]


def tail(gated, carry, rates, gain, direct, gate, pitch):
    rows, width = gate.shape
    poles = rates.shape[0] // pitch
    f32 = jnp.float32
    return call(
        functools.partial(tail_kernel, width // HD, pitch),
        (
            jax.ShapeDtypeStruct((width // HD, rows, HD), f32),
            jax.ShapeDtypeStruct((1, rows), f32),
        ),
        3000 * poles * rows * width,
        10 * rows * width,
        in_specs=[HBM] + [VMEM] * 4 + [HBM],
        scratch_shapes=[
            pltpu.VMEM((rows * pitch, HD), f32),
            pltpu.VMEM((rows * pitch, HD), f32),
            pltpu.VMEM((rows, width), gate.dtype),
            pltpu.SemaphoreType.DMA((4 if rows % 32 == 0 else 1,)),
            pltpu.SemaphoreType.DMA,
        ],
    )(far(gated), carry, rates, gain, direct, far(gate))


def places(runs):
    index = lax.axis_index("seq")
    return index // PLANE % runs, index % PLANE


def norm_kernel(channels, conv, squares, *outs):
    runs, rows, _ = outs[0].shape
    run, place = places(runs)
    scale = lax.rsqrt(squares[...] / channels + 1e-06)
    scale = jnp.transpose(jnp.broadcast_to(scale, (HD, rows)))
    for j in range(PLANE):
        for k in range(runs):
            outs[j][k] = (conv[(run ^ k) * PLANE + (place ^ j)] * scale).astype(outs[j].dtype)


def normalize(conv, squares, channels):
    heads, rows, _ = conv.shape
    message = jax.ShapeDtypeStruct((heads // PLANE, rows, HD), jnp.bfloat16)
    return call(
        functools.partial(norm_kernel, channels),
        (message,) * PLANE,
        heads * rows * HD,
        6 * heads * rows * HD,
    )(conv, squares)


def prefix_state(summary, rates, block_rows, axis):
    size = lax.axis_size(axis)
    place = lax.axis_index(axis)
    span = rates * jnp.float32(block_rows)

    def fade(blocks):
        return jnp.exp(-span * jnp.maximum(blocks, 0).astype(jnp.float32))

    strides = [1]
    while strides[-1] * 4 < size:
        strides.append(strides[-1] * 4)
    before, above = None, size
    for stride in reversed(strides):
        many = above // stride
        digit, inside = place // stride % many, place % above
        total = None if before is None else fade(digit * stride) * before
        for k in range(1, many):
            other = digit ^ k
            gap = other * stride - inside - 1
            sent = summary
            if before is not None:
                sent = fade(other * stride) * before + jnp.where(
                    digit < other, fade(gap) * summary, 0.0
                )
            got = lax.ppermute(sent, axis, [(i, i ^ (stride * k)) for i in range(size)])
            if before is None:
                gap = digit * stride - (inside - digit * stride + other * stride) - 1
                got = jnp.where(other < digit, fade(gap) * got, 0.0)
            total = got if total is None else total + got
        before, above = total, stride
    return before


def attend_kernel(block, pair, *refs):
    *parts, out, scores, values = refs
    _, runs, twice, _ = pair.shape
    rows = twice // 2
    per_block = block // rows
    turns = runs * PLANE // per_block
    own_run, own_place = places(runs)
    factor = LOG2E * HD ** (-0.5)
    row = lax.broadcasted_iota(jnp.int32, (block, block), 0)
    col = lax.broadcasted_iota(jnp.int32, (block, block), 1)
    visible = col <= row
    for k, part in enumerate(parts):
        for j in range(PLANE):
            values[own_run ^ k, own_place ^ j] = part[j]

    def piece(turn, first):
        run, inside = divmod(turn * per_block, PLANE)
        got = [pair[inside + i, run, first : first + rows, :] for i in range(per_block)]
        return jnp.concatenate(got, axis=0)

    def score(turn, part, top):
        got = lax.dot_general(
            piece(turn, 0),
            piece(part, rows),
            (((1,), (1,)), ((), ())),
            preferred_element_type=jnp.float32,
        )
        if part == turn:
            got = jnp.where(visible, got, -1e30)
        scores[turn % 2, :, part * block : (part + 1) * block] = got
        for lane in range(0, block, HD):
            one = got[:, lane : lane + HD]
            top = one if top is None else jnp.maximum(top, one)
        return top

    def weigh(turn, part, top, total, mixed):
        got = scores[turn % 2, :, part * block : (part + 1) * block]
        expo = jnp.exp2(got * factor - top)
        for lane in range(0, block, HD):
            total = total + expo[:, lane : lane + HD]
        run, inside = divmod(part * per_block, PLANE)
        value = values[run, inside : inside + per_block].reshape(block, HD)
        mixed = mixed + jnp.dot(
            expo.astype(jnp.bfloat16), value, preferred_element_type=jnp.float32
        )
        return total, mixed

    zero = jnp.zeros((block, HD), jnp.float32)
    top = score(0, 0, None)
    for turn in range(turns):
        peak = jnp.max(top, axis=1, keepdims=True) * factor
        top, total, mixed = None, zero, zero
        for part in range(turn + 2):
            if turn + 1 < turns:
                top = score(turn + 1, part, top)
            if part <= turn:
                total, mixed = weigh(turn, part, peak, total, mixed)
        mixed = mixed / jnp.sum(total, axis=1, keepdims=True)
        out[turn * per_block : (turn + 1) * per_block] = mixed.astype(out.dtype).reshape(
            per_block, rows, HD
        )


def attend(pair, parts):
    _, runs, twice, _ = pair.shape
    rows = twice // 2
    block = rows
    while block < 512 and PLANE * rows % (2 * block) == 0:
        block *= 2
    length = runs * PLANE * rows
    return call(
        functools.partial(attend_kernel, block),
        jax.ShapeDtypeStruct((runs * PLANE, rows, HD), jnp.bfloat16),
        2 * length * length * HD,
        8 * length * HD,
        length * length // 2,
        scratch_shapes=[
            pltpu.VMEM((2, block, length), jnp.float32),
            pltpu.VMEM((runs, PLANE, rows, HD), jnp.bfloat16),
        ],
    )(pair, *parts)


def gathered_head(query, key, value, first_row):
    count, step = key.shape[0], math.gcd(key.shape[0], 1024)
    query_pos = first_row + jnp.arange(query.shape[0], dtype=jnp.int32)

    def one(turn, carried):
        top, total, mixed = carried
        keys = lax.dynamic_slice_in_dim(key, turn * step, step, 0)
        values = lax.dynamic_slice_in_dim(value, turn * step, step, 0)
        scores = jnp.dot(query, keys.T, preferred_element_type=jnp.float32) * HD ** (-0.5)
        visible = (turn * step + jnp.arange(step, dtype=jnp.int32))[None, :] <= query_pos[:, None]
        scores = jnp.where(visible, scores, -1e30)
        new_top = jnp.maximum(top, jnp.max(scores, axis=1, keepdims=True))
        rescale = jnp.exp(top - new_top)
        expo = jnp.where(visible, jnp.exp(scores - new_top), 0.0)
        total = total * rescale + jnp.sum(expo, axis=1, keepdims=True)
        part = jnp.dot(expo.astype(jnp.bfloat16), values, preferred_element_type=jnp.float32)
        return new_top, total, mixed * rescale + part

    rows = query.shape[0]
    start = (
        jnp.full((rows, 1), -1e30, jnp.float32),
        jnp.zeros((rows, 1), jnp.float32),
        jnp.zeros((rows, HD), jnp.float32),
    )
    _, total, mixed = lax.fori_loop(0, count // step, one, start)
    return (mixed / total).astype(jnp.bfloat16)


def local(
    gate_outer, gate_inner, value_in, pole_rates, pole_weights, skip_gain, query_rows, key_rows
):
    rows, width = gate_outer.shape
    heads = width // HD
    size = lax.axis_size("seq")
    channels = width * lax.axis_size("chan")
    group_count = size // heads
    runs = heads // PLANE
    pitch = -(-heads // 8) * 8

    def exchange(array, members, stride=1):
        if members == 1:
            return array
        span = members * stride
        teams = [
            list(range(first + offset, first + span, stride))
            for first in range(0, size, span)
            for offset in range(stride)
        ]
        return lax.all_to_all(
            array, "seq", 0, 0, axis_index_groups=teams if members < size else None
        )

    def swap(array, distance):
        if distance == 0:
            return array
        return lax.ppermute(array, "seq", [(i, i ^ distance) for i in range(size)])

    gated, summary, rates, gain, direct, chunks = first(
        gate_inner, value_in, pole_rates, pole_weights, skip_gain[None, :], query_rows, key_rows, pitch
    )
    pair = exchange(chunks.reshape(runs, PLANE, 2 * rows, HD), runs, PLANE)
    carry = prefix_state(summary, rates, rows, "seq")
    conv, squares = tail(gated, carry, rates, gain, direct, gate_outer, pitch)
    messages = normalize(conv, lax.psum(squares, "chan"), channels)
    near = [swap(message, j) for j, message in enumerate(messages)]
    values = [swap(jnp.stack([part[k] for part in near]), k * PLANE) for k in range(runs)]
    pair = exchange(jnp.swapaxes(pair, 0, 1), PLANE)
    if group_count == 1:
        mixed = attend(pair, values)
    else:
        mine = lax.axis_index("seq") // heads
        others = [list(range(h, size, heads)) for h in range(heads)]
        gather = functools.partial(
            lax.all_gather, axis_name="seq", axis_index_groups=others, tiled=True
        )
        span = heads * rows
        run, place = places(runs)
        values = [
            jnp.stack(values)[run ^ (h // PLANE), place ^ (h % PLANE)] for h in range(heads)
        ]
        pair = jnp.swapaxes(pair, 0, 1)
        mixed = gathered_head(
            pair[:, :, :rows].reshape(span, HD),
            gather(pair[:, :, rows:].reshape(span, HD)),
            gather(jnp.concatenate(values)),
            mine * span,
        ).reshape(heads, rows, HD)
    return join_heads(exchange(mixed, heads))


def solution(mesh):
    rows = P("seq", "chan")
    poles = P(None, "chan")
    return jax.shard_map(
        local,
        mesh=mesh,
        in_specs=(rows, rows, rows, poles, poles, P("chan"), rows, rows),
        out_specs=rows,
        check_vma=False,
    )
```
